32 devices in a mesh: gop: 4 (over z), row: 8 (over y, x, core).
Axes of the slice: x: 2, y: 2, z: 4, core: 2. Of those that a mesh axis runs over, the one named last changes fastest.
Arguments:
- features: bfloat16 [4, 256, 480, 128], P('gop', 'row'), may hold values from -6 to 6
- filters: bfloat16 [3, 256, 2, 480, 128], P(None, None, None, 'row'), may hold values from -2.390625 to 2.390625
- anchors: int32 [4, 2], replicated, may hold values from 0 to 3, as said below
Outputs:
- joined: bfloat16 [4, 256, 480, 128], P('gop', 'row')
The draws below stay inside these ranges and needn't reach their ends.
Inputs may be any that keep to these rules, and one draw needn't show every extreme that they name: anchors[:, 0] lists each of the 4 frames exactly once; anchors[:, 1] takes exactly two distinct values, each in half of the rows.
All inputs are finite; a program needn't handle non-finite values.
Results may differ from the reference program's by a relative error of at most 0.0062.
Values may be sent and summed in bfloat16 or wider, within the bound.
A program may use at most 256 MiB of HBM per device.

```python
import math
import jax
import jax.numpy as jnp
from jax import lax

C = 128
H = 256
W = 480
FRAMES = 4


def draw_anchors(key, part):
    key_first = jax.random.fold_in(key, 11)
    key_hubs = jax.random.fold_in(key, 12)
    key_sides = jax.random.fold_in(key, 13)
    first_col = jax.random.permutation(key_first, FRAMES).astype(jnp.int32)
    hub_frames = jax.random.permutation(key_hubs, FRAMES)[:2].astype(jnp.int32)
    sides = (jax.random.permutation(key_sides, FRAMES) < FRAMES // 2).astype(jnp.int32)
    second_col = hub_frames[sides]
    return jnp.stack([first_col, second_col], axis=1).astype(jnp.int32)


def levels(rng, dims, split, low, top_value):
    loudness, own = 1.0, jax.random.fold_in(rng, 6)
    for axis_at, shards_of in split:
        draws = jnp.exp(jax.random.uniform(jax.random.fold_in(own, axis_at), (shards_of,), jnp.float32, low / len(split), top_value / len(split)))
        loudness = loudness * jnp.repeat(draws, dims[axis_at] // shards_of).reshape([-1 if axis == axis_at else 1 for axis in range(len(dims))])
    return loudness


def gaussian(rng, shape, deviation, bound, shards=(), kind=jnp.bfloat16):
    drawn = deviation * jax.random.normal(rng, shape, jnp.float32)
    if shards:
        drawn = drawn * levels(rng, shape, shards, -0.22, 0.18)
    return jnp.clip(drawn, -bound, bound).astype(kind)


def setup_inputs(seed: int = 0) -> dict:
    splits = jax.random.split(jax.random.key(seed), 4)
    features = gaussian(splits[0], (FRAMES, H, W, C), 1.0, 6.0, ((0, 4), (1, 8)))
    filters = gaussian(splits[1], (3, H, 2, W, C), 0.4, 2.390625, ((3, 8),))
    anchors = draw_anchors(jax.random.fold_in(splits[3], 71), 0)
    return {"features": features, "filters": filters, "anchors": anchors}


def row_table(length):
    across = jnp.arange(length, dtype=jnp.int32)
    phases = across[:, None] * across[None, :] % length
    angles = phases.astype(jnp.float32) * (2.0 * math.pi / length)
    factor = 1.0 / math.sqrt(length)
    return jnp.concatenate([jnp.cos(angles) * factor, -jnp.sin(angles) * factor], axis=1).astype(jnp.bfloat16)

def column_matrix(length, sign):
    across = jnp.arange(length, dtype=jnp.int32)
    phases = across[:, None] * across[None, :] % length
    angles = phases.astype(jnp.float32) * (2.0 * math.pi / length)
    factor = 1.0 / math.sqrt(length)
    cosine = jnp.cos(angles) * factor
    sine_part = sign * jnp.sin(angles) * factor
    upper = jnp.stack([cosine, -sine_part], axis=-1)
    lower = jnp.stack([sine_part, cosine], axis=-1)
    return jnp.stack([upper, lower], axis=1).reshape(2 * length, 2 * length).astype(jnp.bfloat16)

def reference(features, filters, anchors):
    forward_rows = row_table(W)
    rows_wide = forward_rows.astype(jnp.float32)
    forward_cols = column_matrix(H, -1.0)
    inverse_cols = column_matrix(H, 1.0)
    filt_wide = filters.astype(jnp.float32)

    def spectrum(frame):
        rowwise = jnp.einsum('hwc,wk->hkc', frame.astype(jnp.float32), rows_wide).astype(jnp.bfloat16)
        stacked = rowwise.reshape(2 * H, W * C)
        result = jnp.dot(forward_cols, stacked, preferred_element_type=jnp.float32)
        return result.astype(jnp.bfloat16).reshape(H, 2, W, C)
    spectra = lax.map(spectrum, features)

    def output_frame(number):
        sources = (spectra[number], spectra[anchors[number, 0]], spectra[anchors[number, 1]])
        real_part = jnp.zeros((H, W, C), jnp.float32)
        imag_part = jnp.zeros((H, W, C), jnp.float32)
        for which_one in range(3):
            source_real = sources[which_one][:, 0].astype(jnp.float32)
            source_imag = sources[which_one][:, 1].astype(jnp.float32)
            gain_real = filt_wide[which_one, :, 0]
            gain_imag = filt_wide[which_one, :, 1]
            real_part = real_part + gain_real * source_real - gain_imag * source_imag
            imag_part = imag_part + gain_real * source_imag + gain_imag * source_real
        mixed = jnp.stack([real_part, imag_part], axis=1).astype(jnp.bfloat16)
        back = jnp.dot(inverse_cols, mixed.reshape(2 * H, W * C), preferred_element_type=jnp.float32)
        back = lax.optimization_barrier(back.astype(jnp.bfloat16))
        spatial = jnp.einsum('hkc,wk->hwc', back.reshape(H, 2 * W, C).astype(jnp.float32), rows_wide)
        return (features[number].astype(jnp.float32) + spatial).astype(jnp.bfloat16)
    return lax.map(output_frame, jnp.arange(FRAMES, dtype=jnp.int32))
```

```python
import functools
import math

import jax
import jax.numpy as jnp
import ml_dtypes
import numpy as np
from jax import lax
from jax.experimental import pallas as pl
from jax.experimental.pallas import tpu as pltpu
from jax.sharding import PartitionSpec as P

WINDOW = 8
VMEM_LIMIT = 56 * 1024 * 1024


def trig(length, first, second):
    phases = (first[:, None].astype(np.int64) * second[None, :]) % length
    angles = phases.astype(np.float32) * np.float32(2.0 * math.pi / length)
    factor = np.float32(1.0 / math.sqrt(length))
    return np.cos(angles) * factor, np.sin(angles) * factor


def layout(gops, rows, width):
    per_row = width // rows
    each = -(-(per_row + 1) // (2 * gops))
    columns = []
    for g in range(gops):
        for r in range(rows):
            second = r >= rows // 2
            pair = rows - 1 - r if second else r
            for i in range(each):
                s = 2 * each * g + (each if second else 0) + i
                columns.append(per_row * pair + s if s <= per_row else -1)
    return each, np.array(columns)


def row_rows(gops, rows, width):
    each, columns = layout(gops, rows, width)
    cosine, sine = trig(width, np.maximum(columns, 0), np.arange(width))
    table = np.stack([cosine, -sine], axis=1) * (columns >= 0)[:, None, None]
    return table.reshape(2 * len(columns), width).astype(ml_dtypes.bfloat16)


def column_matrix(length, sign):
    across = np.arange(length)
    cosine, sine = trig(length, across, across)
    sine = np.float32(sign) * sine
    return np.block([[cosine, -sine], [sine, cosine]]).astype(ml_dtypes.bfloat16)


def forward_kernel(rows_each, table_ref, x_ref, o_ref, turned):
    for h in range(0, rows_each, 2):
        pair = jnp.concatenate([x_ref[h], x_ref[h + 1]], axis=1)
        done = jnp.dot(table_ref[...], pair, preferred_element_type=jnp.float32)
        count = done.shape[0]
        turned[pl.ds(h, count, stride=rows_each), :] = done[:, :128]
        turned[pl.ds(h + 1, count, stride=rows_each), :] = done[:, 128:]
    o_ref[...] = turned[...].astype(jnp.bfloat16).reshape(o_ref.shape)


def forward_rows(table, x):
    h, w, c = x.shape
    count = table.shape[0]
    block = 16
    return pl.pallas_call(
        functools.partial(forward_kernel, block),
        grid=(h // block,),
        in_specs=[
            pl.BlockSpec((count, w), lambda i: (0, 0)),
            pl.BlockSpec((block, w, c), lambda i: (i, 0, 0)),
        ],
        out_specs=pl.BlockSpec((count, block, c), lambda i: (0, i, 0)),
        out_shape=jax.ShapeDtypeStruct((count, h, c), jnp.bfloat16),
        scratch_shapes=[pltpu.VMEM((count * block, c), jnp.float32)],
        compiler_params=pltpu.CompilerParams(vmem_limit_bytes=VMEM_LIMIT),
    )(table, x)


def inverse_kernel(rows_each, table_ref, b_ref, x_ref, o_ref, turned):
    turned[...] = b_ref[...].reshape(turned.shape).astype(jnp.float32)
    count = table_ref.shape[1]
    for h in range(0, rows_each, 2):
        pair = jnp.concatenate(
            [turned[pl.ds(h + d, count, stride=rows_each), :] for d in range(2)], axis=1
        ).astype(jnp.bfloat16)
        done = jnp.dot(table_ref[...], pair, preferred_element_type=jnp.float32)
        for d in range(2):
            added = x_ref[h + d].astype(jnp.float32) + done[:, 128 * d : 128 * d + 128]
            o_ref[h + d] = added.astype(jnp.bfloat16)


def inverse_rows(table, back, x):
    h, w, c = x.shape
    count = table.shape[1]
    block = 16
    return pl.pallas_call(
        functools.partial(inverse_kernel, block),
        grid=(h // block,),
        in_specs=[
            pl.BlockSpec((w, count), lambda i: (0, 0)),
            pl.BlockSpec((count, block, c), lambda i: (0, i, 0)),
            pl.BlockSpec((block, w, c), lambda i: (i, 0, 0)),
        ],
        out_specs=pl.BlockSpec((block, w, c), lambda i: (i, 0, 0)),
        out_shape=jax.ShapeDtypeStruct((h, w, c), jnp.bfloat16),
        scratch_shapes=[pltpu.VMEM((count * block, c), jnp.float32)],
        compiler_params=pltpu.CompilerParams(vmem_limit_bytes=VMEM_LIMIT),
    )(table, back, x)


def middle_kernel(
    frames, rows, height,
    place_ref, weight_ref, anchor_ref, x_ref, p_ref, n_ref, mf_ref, mi_ref, o_ref,
    p_wide, n_wide, spec, mixed,
):
    slot = pl.program_id(0)
    lines = 2 * WINDOW

    @pl.when(slot == 0)
    def _():
        def widen(k, carry):
            mirror = lax.rem(height - k, height)
            for j in range(3):
                at = pl.ds(pl.multiple_of((j * height + k) * lines, lines), lines)
                p_wide[at, :] = p_ref[j, k].astype(jnp.float32)
                n_wide[at, :] = n_ref[j, mirror].astype(jnp.float32)
            return carry

        lax.fori_loop(0, height, widen, 0, unroll=4)

    short = x_ref.shape[2]
    for f in range(0, frames, 2):
        sides = []
        for d in range(2):
            sides.append(
                jnp.concatenate(
                    [x_ref[(f + d) * rows + r, q] for q in range(2) for r in range(rows)], axis=0
                )
            )
        done = jnp.dot(
            mf_ref[...], jnp.concatenate(sides, axis=1), preferred_element_type=jnp.float32
        ).astype(jnp.bfloat16)
        spec[f] = done[:, :128]
        spec[f + 1] = done[:, 128:]

    place_p, place_n = place_ref[0, slot], place_ref[1, slot]
    weight_p, weight_n = weight_ref[0, slot], weight_ref[1, slot]
    chunk = 32

    def mix(step, carry):
        k = pl.multiple_of(step * chunk, chunk)
        gains = []
        for j in range(3):
            parts = []
            for p in range(2):
                start = (j * height + k) * lines + p * WINDOW
                right = p_wide[pl.ds(start + place_p, chunk, stride=lines), :]
                left = n_wide[pl.ds(start + place_n, chunk, stride=lines), :]
                left = left * weight_n
                parts.append(right * weight_p + (left if p == 0 else -left))
            gains.append(parts)
        for f in range(frames):
            real, imag = None, None
            for j in range(3):
                source = f if j == 0 else anchor_ref[f, j - 1]
                s_real = spec[source, pl.ds(k, chunk), :].astype(jnp.float32)
                s_imag = spec[source, pl.ds(height + k, chunk), :].astype(jnp.float32)
                g_real, g_imag = gains[j]
                new_real = g_real * s_real - g_imag * s_imag
                new_imag = g_real * s_imag + g_imag * s_real
                real = new_real if real is None else real + new_real
                imag = new_imag if imag is None else imag + new_imag
            lanes = pl.ds(f * 128, 128)
            mixed[pl.ds(k, chunk), lanes] = real.astype(jnp.bfloat16)
            mixed[pl.ds(height + k, chunk), lanes] = imag.astype(jnp.bfloat16)
        return carry

    lax.fori_loop(0, height // chunk, mix, 0)

    for f in range(0, frames, 2):
        back = jnp.dot(
            mi_ref[...], mixed[:, 128 * f : 128 * f + 256], preferred_element_type=jnp.float32
        ).astype(jnp.bfloat16)
        for d in range(2):
            for q in range(2):
                for r in range(rows):
                    at = q * height + r * short
                    o_ref[(f + d) * rows + r, q] = back[at : at + short, 128 * d : 128 * d + 128]


def middle(frames, rows, place, weight, anchors, x, plus, minus, mf, mi):
    n, count, short, c = x.shape
    height = plus.shape[1]
    whole = lambda shape: pl.BlockSpec(shape, lambda i: (0,) * len(shape))
    smem = pl.BlockSpec(memory_space=pltpu.SMEM)
    block = pl.BlockSpec((n, 2, short, c), lambda i: (0, i, 0, 0))
    return pl.pallas_call(
        functools.partial(middle_kernel, frames, rows, height),
        grid=(count // 2,),
        in_specs=[smem, smem, smem, block, whole(plus.shape), whole(minus.shape),
                  whole(mf.shape), whole(mi.shape)],
        out_specs=block,
        out_shape=jax.ShapeDtypeStruct(x.shape, jnp.bfloat16),
        scratch_shapes=[
            pltpu.VMEM((3 * height * 2 * WINDOW, c), jnp.float32),
            pltpu.VMEM((3 * height * 2 * WINDOW, c), jnp.float32),
            pltpu.VMEM((frames, 2 * height, c), jnp.bfloat16),
            pltpu.VMEM((2 * height, frames * c), jnp.bfloat16),
        ],
        compiler_params=pltpu.CompilerParams(vmem_limit_bytes=VMEM_LIMIT),
    )(place, weight, anchors, x, plus, minus, mf, mi)


def on_device(gops, rows, features, filters, anchors):
    h, w, c = features.shape[1:]
    height = filters.shape[1]
    per_row = filters.shape[3]
    devices = gops * rows
    table = row_rows(gops, rows, w)
    each, _ = layout(gops, rows, w)
    g, r = lax.axis_index("gop"), lax.axis_index("row")
    second = r >= rows // 2

    slots = 2 * each * g + jnp.where(second, each, 0) + jnp.arange(each)
    theirs = 2 * each * g + jnp.where(second, 0, each) + jnp.arange(each)
    limit = per_row - WINDOW
    start_plus = lambda s: jnp.clip(s[0], 0, limit)
    start_minus = lambda s: jnp.clip(per_row - s[each - 1], 0, limit)
    cut = lambda start: lax.dynamic_slice_in_dim(filters, start, WINDOW, 3).reshape(
        3, height, 2 * WINDOW, c
    )
    to_send = cut(jnp.where(second, start_minus(theirs), start_plus(theirs)))
    got = lax.ppermute(to_send, "row", [(i, rows - 1 - i) for i in range(rows)])
    own = cut(jnp.where(second, start_minus(slots), start_plus(slots)))
    plus = jnp.where(second, got, own)
    minus = jnp.where(second, own, got)
    place = jnp.stack([slots - start_plus(slots), per_row - slots - start_minus(slots)])
    place = jnp.clip(place, 0, WINDOW - 1).astype(jnp.int32)
    weight = jnp.stack([slots < per_row, (slots >= 1) & (slots <= per_row)]).astype(jnp.float32)

    done = forward_rows(jnp.asarray(table), features[0])
    slab = lax.all_to_all(
        done.reshape(devices, 2 * each, h, c), ("gop", "row"), split_axis=0, concat_axis=0, tiled=True
    )
    back = middle(
        gops, rows, place, weight, anchors, slab, plus, minus,
        jnp.asarray(column_matrix(height, -1.0)), jnp.asarray(column_matrix(height, 1.0)),
    )
    back = lax.all_to_all(back, ("gop", "row"), split_axis=0, concat_axis=0, tiled=True)
    joined = inverse_rows(jnp.asarray(table.T), back.reshape(devices * 2 * each, h, c), features[0])
    return joined[None]


def solution(mesh):
    in_specs = (P("gop", "row", None, None), P(None, None, None, "row", None), P())
    out_specs = P("gop", "row", None, None)
    return jax.shard_map(
        functools.partial(on_device, mesh.shape["gop"], mesh.shape["row"]),
        mesh=mesh, in_specs=in_specs, out_specs=out_specs, check_vma=False,
    )
```

```python
import functools
import math

import jax
import jax.numpy as jnp
import ml_dtypes
import numpy as np
from jax import lax
from jax.experimental import pallas as pl
from jax.experimental.pallas import tpu as pltpu
from jax.sharding import PartitionSpec as P

CHUNKS = 2
VMEM_LIMIT = 56 * 1024 * 1024


def cost(flops, moved):
    return pl.CostEstimate(flops=flops, bytes_accessed=moved, transcendentals=0)


def trig(length, first, second):
    phases = (first[:, None].astype(np.int64) * second[None, :]) % length
    angles = phases.astype(np.float32) * np.float32(2.0 * math.pi / length)
    factor = np.float32(1.0 / math.sqrt(length))
    return np.cos(angles) * factor, np.sin(angles) * factor


def layout(gops, rows, width):
    per_row = width // rows
    each = -(-(per_row + 1) // (2 * gops))
    columns = []
    for g in range(gops):
        for r in range(rows):
            second = r >= rows // 2
            pair = rows - 1 - r if second else r
            for i in range(each):
                s = 2 * each * g + (each if second else 0) + i
                columns.append(per_row * pair + s if s <= per_row else -1)
    return each, np.array(columns)


def row_rows(gops, rows, width):
    each, columns = layout(gops, rows, width)
    cosine, sine = trig(width, np.maximum(columns, 0), np.arange(width))
    table = np.stack([cosine, -sine], axis=1) * (columns >= 0)[:, None, None]
    return table.reshape(2 * len(columns), width).astype(ml_dtypes.bfloat16)


def column_matrix(length, sign):
    across = np.arange(length)
    cosine, sine = trig(length, across, across)
    sine = np.float32(sign) * sine
    return np.block([[cosine, -sine], [sine, cosine]]).astype(ml_dtypes.bfloat16)


def forward_kernel(rows_each, table_ref, x_ref, o_ref, turned):
    for h in range(0, rows_each, 2):
        pair = jnp.concatenate([x_ref[h], x_ref[h + 1]], axis=1)
        done = jnp.dot(table_ref[...], pair, preferred_element_type=jnp.float32)
        count = done.shape[0]
        turned[pl.ds(h, count, stride=rows_each), :] = done[:, :128]
        turned[pl.ds(h + 1, count, stride=rows_each), :] = done[:, 128:]
    o_ref[...] = turned[...].astype(jnp.bfloat16).reshape(o_ref.shape)


def forward_rows(table, x):
    h, w, c = x.shape
    count = table.shape[0]
    block = 16
    return pl.pallas_call(
        functools.partial(forward_kernel, block),
        grid=(h // block,),
        in_specs=[
            pl.BlockSpec((count, w), lambda i: (0, 0)),
            pl.BlockSpec((block, w, c), lambda i: (i, 0, 0)),
        ],
        out_specs=pl.BlockSpec((count, block, c), lambda i: (0, i, 0)),
        out_shape=jax.ShapeDtypeStruct((count, h, c), jnp.bfloat16),
        scratch_shapes=[pltpu.VMEM((count * block, c), jnp.float32)],
        cost_estimate=cost(2 * count * w * h * c, 2 * h * c * (w + count)),
        compiler_params=pltpu.CompilerParams(vmem_limit_bytes=VMEM_LIMIT),
    )(table, x)


def inverse_kernel(rows_each, chunks, table_ref, *refs):
    b_refs, (x_ref, o_ref, turned) = refs[:chunks], refs[chunks:]
    count = table_ref.shape[1]
    part = count // chunks * rows_each
    for n in range(chunks):
        wide = b_refs[n][...].reshape(part, 128).astype(jnp.float32)
        turned[n * part : n * part + part, :] = wide
    for h in range(0, rows_each, 2):
        pair = jnp.concatenate(
            [turned[pl.ds(h + d, count, stride=rows_each), :] for d in range(2)], axis=1
        ).astype(jnp.bfloat16)
        done = jnp.dot(table_ref[...], pair, preferred_element_type=jnp.float32)
        for d in range(2):
            added = x_ref[h + d].astype(jnp.float32) + done[:, 128 * d : 128 * d + 128]
            o_ref[h + d] = added.astype(jnp.bfloat16)


def inverse_rows(table, backs, x):
    h, w, c = x.shape
    count = table.shape[1]
    chunks = len(backs)
    block = 16
    return pl.pallas_call(
        functools.partial(inverse_kernel, block, chunks),
        grid=(h // block,),
        in_specs=[
            pl.BlockSpec((w, count), lambda i: (0, 0)),
            *[pl.BlockSpec((count // chunks, block, c), lambda i: (0, i, 0))] * chunks,
            pl.BlockSpec((block, w, c), lambda i: (i, 0, 0)),
        ],
        out_specs=pl.BlockSpec((block, w, c), lambda i: (i, 0, 0)),
        out_shape=jax.ShapeDtypeStruct((h, w, c), jnp.bfloat16),
        scratch_shapes=[pltpu.VMEM((count * block, c), jnp.float32)],
        cost_estimate=cost(2 * count * w * h * c, 2 * h * c * (2 * w + count)),
        compiler_params=pltpu.CompilerParams(vmem_limit_bytes=VMEM_LIMIT),
    )(table, *backs, x)


def middle_kernel(
    frames, rows, height, window,
    place_ref, weight_ref, anchor_ref, x_ref, p_ref, n_ref, mf_ref, mi_ref, o_ref,
    p_wide, n_wide, n_plain, spec, mixed,
):
    slot = pl.program_id(0)
    lines = 2 * window

    @pl.when(slot == 0)
    def _():
        p_wide[...] = p_ref[...].astype(jnp.float32)
        n_plain[...] = n_ref[...].astype(jnp.float32)

        def mirror(k, carry):
            there = lax.rem(height - k, height)
            for j in range(3):
                to = pl.ds(pl.multiple_of((j * height + k) * lines, lines), lines)
                at = pl.ds(pl.multiple_of((j * height + there) * lines, lines), lines)
                n_wide[to, :] = n_plain[at, :]
            return carry

        lax.fori_loop(0, height, mirror, 0, unroll=4)

    short = x_ref.shape[2]
    for f in range(0, frames, 2):
        sides = []
        for d in range(2):
            sides.append(
                jnp.concatenate(
                    [x_ref[(f + d) * rows + r, q] for q in range(2) for r in range(rows)], axis=0
                )
            )
        done = jnp.dot(
            mf_ref[...], jnp.concatenate(sides, axis=1), preferred_element_type=jnp.float32
        ).astype(jnp.bfloat16)
        spec[f] = done[:, :128]
        spec[f + 1] = done[:, 128:]

    place_p, place_n = place_ref[0, slot], place_ref[1, slot]
    weight_p, weight_n = weight_ref[0, slot], weight_ref[1, slot]
    chunk = 32

    def mix(step, carry):
        k = pl.multiple_of(step * chunk, chunk)
        gains = []
        for j in range(3):
            parts = []
            for p in range(2):
                start = (j * height + k) * lines + p * window
                right = p_wide[pl.ds(start + place_p, chunk, stride=lines), :]
                left = n_wide[pl.ds(start + place_n, chunk, stride=lines), :]
                left = left * weight_n
                parts.append(right * weight_p + (left if p == 0 else -left))
            gains.append(parts)
        for f in range(frames):
            real, imag = None, None
            for j in range(3):
                source = f if j == 0 else anchor_ref[f, j - 1]
                s_real = spec[source, pl.ds(k, chunk), :].astype(jnp.float32)
                s_imag = spec[source, pl.ds(height + k, chunk), :].astype(jnp.float32)
                g_real, g_imag = gains[j]
                new_real = g_real * s_real - g_imag * s_imag
                new_imag = g_real * s_imag + g_imag * s_real
                real = new_real if real is None else real + new_real
                imag = new_imag if imag is None else imag + new_imag
            lanes = pl.ds(f * 128, 128)
            mixed[pl.ds(k, chunk), lanes] = real.astype(jnp.bfloat16)
            mixed[pl.ds(height + k, chunk), lanes] = imag.astype(jnp.bfloat16)
        return carry

    lax.fori_loop(0, height // chunk, mix, 0)

    for f in range(0, frames, 2):
        back = jnp.dot(
            mi_ref[...], mixed[:, 128 * f : 128 * f + 256], preferred_element_type=jnp.float32
        ).astype(jnp.bfloat16)
        for d in range(2):
            for q in range(2):
                for r in range(rows):
                    at = q * height + r * short
                    o_ref[(f + d) * rows + r, q] = back[at : at + short, 128 * d : 128 * d + 128]


def middle(frames, rows, height, window, place, weight, anchors, x, plus, minus, mf, mi):
    n, count, short, c = x.shape
    whole = lambda shape: pl.BlockSpec(shape, lambda i: (0,) * len(shape))
    smem = pl.BlockSpec(memory_space=pltpu.SMEM)
    block = pl.BlockSpec((n, 2, short, c), lambda i: (0, i, 0, 0))
    return pl.pallas_call(
        functools.partial(middle_kernel, frames, rows, height, window),
        grid=(count // 2,),
        in_specs=[smem, smem, smem, block, whole(plus.shape), whole(minus.shape),
                  whole(mf.shape), whole(mi.shape)],
        out_specs=block,
        out_shape=jax.ShapeDtypeStruct(x.shape, jnp.bfloat16),
        scratch_shapes=[
            *[pltpu.VMEM(plus.shape, jnp.float32)] * 3,
            pltpu.VMEM((frames, 2 * height, c), jnp.bfloat16),
            pltpu.VMEM((2 * height, frames * c), jnp.bfloat16),
        ],
        cost_estimate=cost(8 * height * x.size, 4 * x.size + 4 * plus.size),
        compiler_params=pltpu.CompilerParams(vmem_limit_bytes=VMEM_LIMIT),
    )(place, weight, anchors, x, plus, minus, mf, mi)


def on_device(gops, rows, features, filters, anchors):
    h, w, c = features.shape[1:]
    height = filters.shape[1]
    per_row = filters.shape[3]
    devices = gops * rows
    table = row_rows(gops, rows, w)
    each, _ = layout(gops, rows, w)
    g, r = lax.axis_index("gop"), lax.axis_index("row")
    second = r >= rows // 2

    chunks = math.gcd(CHUNKS, each)
    size = each // chunks
    window = max(4, size)
    limit = per_row - window
    start_plus = lambda s: jnp.clip(s[0], 0, limit)
    start_minus = lambda s: jnp.clip(per_row - s[size - 1], 0, limit)
    cut = lambda start: lax.dynamic_slice_in_dim(filters, start, window, 3).reshape(-1, c)
    tables = table.reshape(devices, chunks, 2 * size, w).swapaxes(0, 1).reshape(chunks, -1, w)
    first_slot = 2 * each * g + jnp.where(second, each, 0)
    first_theirs = 2 * each * g + jnp.where(second, 0, each)
    forward = jnp.asarray(column_matrix(height, -1.0))
    inverse = jnp.asarray(column_matrix(height, 1.0))
    swap = lambda x: lax.all_to_all(
        x.reshape(devices, 2 * size, h, c), ("gop", "row"), split_axis=0, concat_axis=0, tiled=True
    )

    gains, slabs = [], []
    x = features[0]
    for n in range(chunks):
        slots = first_slot + n * size + jnp.arange(size)
        theirs = first_theirs + n * size + jnp.arange(size)
        to_send = cut(jnp.where(second, start_minus(theirs), start_plus(theirs)))
        if n == 0:
            x, to_send = lax.optimization_barrier((x, to_send))
        got = lax.ppermute(to_send, "row", [(i, rows - 1 - i) for i in range(rows)])
        own = cut(jnp.where(second, start_minus(slots), start_plus(slots)))
        place = jnp.stack([slots - start_plus(slots), per_row - slots - start_minus(slots)])
        place = jnp.clip(place, 0, window - 1).astype(jnp.int32)
        weight = jnp.stack([slots < per_row, (slots >= 1) & (slots <= per_row)])
        gains.append((place, weight.astype(jnp.float32), own, got))
        slabs.append(swap(forward_rows(jnp.asarray(tables[n]), x)))
    backs = []
    for n in range(chunks):
        place, weight, own, got = gains[n]
        plus = jnp.where(second, got, own)
        minus = jnp.where(second, own, got)
        back = middle(gops, rows, height, window, place, weight, anchors, slabs[n], plus, minus,
                      forward, inverse)
        backs.append(swap(back).reshape(devices * 2 * size, h, c))
    table_back = jnp.asarray(np.ascontiguousarray(tables.reshape(-1, w).T))
    return inverse_rows(table_back, backs, features[0])[None]


def solution(mesh):
    in_specs = (P("gop", "row", None, None), P(None, None, None, "row", None), P())
    out_specs = P("gop", "row", None, None)
    return jax.shard_map(
        functools.partial(on_device, mesh.shape["gop"], mesh.shape["row"]),
        mesh=mesh, in_specs=in_specs, out_specs=out_specs, check_vma=False,
    )
```

```python
import functools
import math

import jax
import jax.numpy as jnp
import ml_dtypes
import numpy as np
from jax import lax
from jax.experimental import pallas as pl
from jax.experimental.pallas import tpu as pltpu
from jax.sharding import PartitionSpec as P

CHUNKS = 4
MESH = pl.DeviceIdType.MESH
VMEM_LIMIT = 56 * 1024 * 1024


def cost(flops, moved):
    return pl.CostEstimate(flops=flops, bytes_accessed=moved, transcendentals=0)


def trig(length, first, second):
    phases = (first[:, None].astype(np.int64) * second[None, :]) % length
    angles = phases.astype(np.float32) * np.float32(2.0 * math.pi / length)
    factor = np.float32(1.0 / math.sqrt(length))
    return np.cos(angles) * factor, np.sin(angles) * factor


def layout(gops, rows, width):
    per_row = width // rows
    each = -(-(per_row + 1) // (2 * gops))
    columns = []
    for g in range(gops):
        for r in range(rows):
            second = r >= rows // 2
            pair = rows - 1 - r if second else r
            for i in range(each):
                s = 2 * each * g + (each if second else 0) + i
                columns.append(per_row * pair + s if s <= per_row else -1)
    return each, np.array(columns)


def row_rows(gops, rows, width):
    each, columns = layout(gops, rows, width)
    cosine, sine = trig(width, np.maximum(columns, 0), np.arange(width))
    table = np.stack([cosine, -sine], axis=1) * (columns >= 0)[:, None, None]
    return table.reshape(2 * len(columns), width).astype(ml_dtypes.bfloat16)


def column_matrix(length, sign):
    across = np.arange(length)
    cosine, sine = trig(length, across, across)
    sine = np.float32(sign) * sine
    return np.block([[cosine, -sine], [sine, cosine]]).astype(ml_dtypes.bfloat16)


def inverse_kernel(rows_each, table_ref, b_ref, x_ref, o_ref, turned):
    turned[...] = b_ref[...].reshape(turned.shape).astype(jnp.float32)
    count = table_ref.shape[1]
    for h in range(0, rows_each, 2):
        pair = jnp.concatenate(
            [turned[pl.ds(h + d, count, stride=rows_each), :] for d in range(2)], axis=1
        ).astype(jnp.bfloat16)
        done = jnp.dot(table_ref[...], pair, preferred_element_type=jnp.float32)
        for d in range(2):
            added = x_ref[h + d].astype(jnp.float32) + done[:, 128 * d : 128 * d + 128]
            o_ref[h + d] = added.astype(jnp.bfloat16)


def inverse_rows(table, back, x):
    h, w, c = x.shape
    count = table.shape[1]
    block = 16
    return pl.pallas_call(
        functools.partial(inverse_kernel, block),
        grid=(h // block,),
        in_specs=[
            pl.BlockSpec((w, count), lambda i: (0, 0)),
            pl.BlockSpec((count, block, c), lambda i: (0, i, 0)),
            pl.BlockSpec((block, w, c), lambda i: (i, 0, 0)),
        ],
        out_specs=pl.BlockSpec((block, w, c), lambda i: (i, 0, 0)),
        out_shape=jax.ShapeDtypeStruct((h, w, c), jnp.bfloat16),
        scratch_shapes=[pltpu.VMEM((count * block, c), jnp.float32)],
        cost_estimate=cost(2 * count * w * h * c, 2 * h * c * (2 * w + count)),
        compiler_params=pltpu.CompilerParams(vmem_limit_bytes=VMEM_LIMIT),
    )(table, back, x)


def exchange_kernel(
    frames, rows, height, chunks, size, parts, fold, window,
    place_ref, weight_ref, anchor_ref, table_ref, x_ref, own_ref, give_ref, mf_ref, mi_ref, o_ref,
    turned, sent, slab, back, got, p_wide, n_wide, n_plain, spec, mixed,
    f_send, f_recv, a_send, a_recv, b_send, b_recv, local_sem,
):
    devices = frames * rows
    g, r = lax.axis_index("gop"), lax.axis_index("row")
    me = g * rows + r
    second = r >= rows // 2
    short = x_ref.shape[0]
    lines = 2 * window

    def target(step):
        to = lax.rem(me + step, devices)
        return to, (to // rows, lax.rem(to, rows))

    barrier = pltpu.get_barrier_semaphore()

    def greet(step, carry):
        _, there = target(step)
        pl.semaphore_signal(barrier, inc=1, device_id=there, device_id_type=MESH)
        return carry

    lax.fori_loop(1, devices, greet, 0)
    pl.semaphore_wait(barrier, devices - 1)

    def gain_copy(part):
        return pltpu.make_async_remote_copy(
            src_ref=give_ref.at[part], dst_ref=got.at[part],
            send_sem=f_send.at[part], recv_sem=f_recv.at[part],
            device_id=(g, rows - 1 - r), device_id_type=MESH,
        )

    for part in range(parts):
        gain_copy(part).start()

    def send_all(n, source, landing, send_sem, recv_sem):
        def one(step, carry):
            to, there = target(step)
            pltpu.make_async_remote_copy(
                src_ref=source.at[n, to], dst_ref=landing.at[n, me],
                send_sem=send_sem.at[n], recv_sem=recv_sem.at[n],
                device_id=there, device_id_type=MESH,
            ).start()
            return carry

        lax.fori_loop(1, devices, one, 0)

    def wait_all(n, ref, sem):
        some = ref.at[n, pl.ds(0, devices - 1)]
        pltpu.make_async_copy(some, some, sem.at[n]).wait()

    count = devices * size * 2

    def forward(n, carry):
        for half in range(short // 16):
            def two(i, inner):
                h = half * 16 + 2 * i
                pair = jnp.concatenate([x_ref[h], x_ref[h + 1]], axis=1)
                done = jnp.dot(table_ref[n], pair, preferred_element_type=jnp.float32)
                turned[pl.ds(2 * i, count, stride=16), :] = done[:, :128]
                turned[pl.ds(2 * i + 1, count, stride=16), :] = done[:, 128:]
                return inner

            lax.fori_loop(0, 8, two, 0, unroll=True)
            sent[n, :, :, pl.ds(half * 16, 16), :] = (
                turned[...].astype(jnp.bfloat16).reshape(devices, 2 * size, 16, 128)
            )
        send_all(n, sent, slab, a_send, a_recv)
        slab[n, me] = sent[n, me]
        return carry

    lax.fori_loop(0, chunks, forward, 0)

    def middle(n, carry):
        @pl.when(lax.rem(n, fold) == 0)
        def _():
            part = n // fold
            gain_copy(part).wait()
            block = 512

            def widen(i, inner):
                at = pl.ds(pl.multiple_of(i * block, block), block)
                own = own_ref[part, at, :].astype(jnp.float32)
                other = got[part, at, :].astype(jnp.float32)
                p_wide[at, :] = jnp.where(second, other, own)
                n_plain[at, :] = jnp.where(second, own, other)
                return inner

            lax.fori_loop(0, 3 * height * lines // block, widen, 0)

            def mirror(k, inner):
                there = lax.rem(height - k, height)
                for j in range(3):
                    to = pl.ds(pl.multiple_of((j * height + k) * lines, lines), lines)
                    at = pl.ds(pl.multiple_of((j * height + there) * lines, lines), lines)
                    n_wide[to, :] = n_plain[at, :]
                return inner

            lax.fori_loop(0, height, mirror, 0)

        wait_all(n, slab, a_recv)

        def one_slot(i, inner):
            slot = n * size + i
            for f in range(0, frames, 2):
                sides = [
                    jnp.concatenate(
                        [slab[n, (f + d) * rows + k, 2 * i + q] for q in range(2) for k in range(rows)],
                        axis=0,
                    )
                    for d in range(2)
                ]
                done = jnp.dot(
                    mf_ref[...], jnp.concatenate(sides, axis=1), preferred_element_type=jnp.float32
                ).astype(jnp.bfloat16)
                spec[f] = done[:, :128]
                spec[f + 1] = done[:, 128:]

            place_p, place_n = place_ref[0, slot], place_ref[1, slot]
            weight_p, weight_n = weight_ref[0, slot], weight_ref[1, slot]
            chunk = 32

            def mix(step, deep):
                k = pl.multiple_of(step * chunk, chunk)
                gains = []
                for j in range(3):
                    pieces = []
                    for p in range(2):
                        start = (j * height + k) * lines + p * window
                        right = p_wide[pl.ds(start + place_p, chunk, stride=lines), :]
                        left = n_wide[pl.ds(start + place_n, chunk, stride=lines), :]
                        left = left * weight_n
                        pieces.append(right * weight_p + (left if p == 0 else -left))
                    gains.append(pieces)
                for f in range(frames):
                    real, imag = None, None
                    for j in range(3):
                        source = f if j == 0 else anchor_ref[f, j - 1]
                        s_real = spec[source, pl.ds(k, chunk), :].astype(jnp.float32)
                        s_imag = spec[source, pl.ds(height + k, chunk), :].astype(jnp.float32)
                        g_real, g_imag = gains[j]
                        new_real = g_real * s_real - g_imag * s_imag
                        new_imag = g_real * s_imag + g_imag * s_real
                        real = new_real if real is None else real + new_real
                        imag = new_imag if imag is None else imag + new_imag
                    lanes = pl.ds(f * 128, 128)
                    mixed[pl.ds(k, chunk), lanes] = real.astype(jnp.bfloat16)
                    mixed[pl.ds(height + k, chunk), lanes] = imag.astype(jnp.bfloat16)
                return deep

            lax.fori_loop(0, height // chunk, mix, 0)

            for f in range(0, frames, 2):
                done = jnp.dot(
                    mi_ref[...], mixed[:, 128 * f : 128 * f + 256],
                    preferred_element_type=jnp.float32,
                ).astype(jnp.bfloat16)
                for d in range(2):
                    for q in range(2):
                        for k in range(rows):
                            at = q * height + k * short
                            back[n, (f + d) * rows + k, 2 * i + q] = done[
                                at : at + short, 128 * d : 128 * d + 128
                            ]
            return inner

        lax.fori_loop(0, size, one_slot, 0)
        send_all(n, back, o_ref, b_send, b_recv)
        pltpu.make_async_copy(back.at[n, me], o_ref.at[n, me], local_sem.at[n]).start()
        return carry

    lax.fori_loop(0, chunks, middle, 0)

    def finish(n, carry):
        wait_all(n, sent, a_send)
        wait_all(n, back, b_send)
        wait_all(n, o_ref, b_recv)
        pltpu.make_async_copy(back.at[n, me], o_ref.at[n, me], local_sem.at[n]).wait()
        return carry

    lax.fori_loop(0, chunks, finish, 0)


def exchange(frames, rows, height, size, fold, window, place, weight, anchors, table, x, own, give, mf, mi):
    chunks, count, w = table.shape
    h, _, c = x.shape
    devices = frames * rows
    parts = own.shape[0]
    shape = (chunks, devices, 2 * size, h, c)
    smem = pl.BlockSpec(memory_space=pltpu.SMEM)
    vmem = pl.BlockSpec(memory_space=pltpu.VMEM)
    hbm = pl.BlockSpec(memory_space=pl.ANY)
    wide = pltpu.VMEM(own.shape[1:], jnp.float32)
    dma = pltpu.SemaphoreType.DMA
    return pl.pallas_call(
        functools.partial(exchange_kernel, frames, rows, height, chunks, size, parts, fold, window),
        in_specs=[smem, smem, smem, vmem, vmem, vmem, hbm, vmem, vmem],
        out_specs=hbm,
        out_shape=jax.ShapeDtypeStruct(shape, jnp.bfloat16),
        scratch_shapes=[
            pltpu.VMEM((count * 16, c), jnp.float32),
            *[pltpu.VMEM(shape, jnp.bfloat16)] * 3,
            pltpu.VMEM(own.shape, jnp.bfloat16),
            wide, wide, wide,
            pltpu.VMEM((frames, 2 * height, c), jnp.bfloat16),
            pltpu.VMEM((2 * height, frames * c), jnp.bfloat16),
            dma((parts,)), dma((parts,)),
            *[dma((chunks,))] * 5,
        ],
        cost_estimate=cost(8 * height * x.size, 4 * x.size + 4 * own.size),
        compiler_params=pltpu.CompilerParams(
            vmem_limit_bytes=VMEM_LIMIT, collective_id=0, has_side_effects=True
        ),
    )(place, weight, anchors, table, x, own, give, mf, mi)


def on_device(gops, rows, features, filters, anchors):
    h, w, c = features.shape[1:]
    height = filters.shape[1]
    per_row = filters.shape[3]
    devices = gops * rows
    table = row_rows(gops, rows, w)
    each, _ = layout(gops, rows, w)
    g, r = lax.axis_index("gop"), lax.axis_index("row")
    second = r >= rows // 2
    window = 4
    parts = max(1, each // window)
    part_size = each // parts
    chunks = math.gcd(CHUNKS, each)
    size = each // chunks
    limit = per_row - window
    start_plus = lambda s: jnp.clip(s[0], 0, limit)
    start_minus = lambda s: jnp.clip(per_row - s[part_size - 1], 0, limit)
    cut = lambda start: lax.dynamic_slice_in_dim(filters, start, window, 3).reshape(-1, c)
    tables = table.reshape(devices, chunks, 2 * size, w).swapaxes(0, 1).reshape(chunks, -1, w)
    first_slot = 2 * each * g + jnp.where(second, each, 0)
    first_theirs = 2 * each * g + jnp.where(second, 0, each)

    give, own, places, weights = [], [], [], []
    for n in range(parts):
        slots = first_slot + n * part_size + jnp.arange(part_size)
        theirs = first_theirs + n * part_size + jnp.arange(part_size)
        give.append(cut(jnp.where(second, start_minus(theirs), start_plus(theirs))))
        own.append(cut(jnp.where(second, start_minus(slots), start_plus(slots))))
        places.append(jnp.stack([slots - start_plus(slots), per_row - slots - start_minus(slots)]))
        weights.append(jnp.stack([slots < per_row, (slots >= 1) & (slots <= per_row)]))
    place = jnp.clip(jnp.concatenate(places, axis=1), 0, window - 1).astype(jnp.int32)
    weight = jnp.concatenate(weights, axis=1).astype(jnp.float32)
    back = exchange(
        gops, rows, height, size, part_size // size, window, place, weight, anchors,
        jnp.asarray(tables), features[0], jnp.stack(own), jnp.stack(give),
        jnp.asarray(column_matrix(height, -1.0)), jnp.asarray(column_matrix(height, 1.0)),
    )
    table_back = jnp.asarray(np.ascontiguousarray(tables.reshape(-1, w).T))
    return inverse_rows(table_back, back.reshape(-1, h, c), features[0])[None]


def solution(mesh):
    in_specs = (P("gop", "row", None, None), P(None, None, None, "row", None), P())
    out_specs = P("gop", "row", None, None)
    return jax.shard_map(
        functools.partial(on_device, mesh.shape["gop"], mesh.shape["row"]),
        mesh=mesh, in_specs=in_specs, out_specs=out_specs, check_vma=False,
    )
```

```python
import functools
import math

import jax
import jax.numpy as jnp
import ml_dtypes
import numpy as np
from jax import lax
from jax.experimental import pallas as pl
from jax.experimental.pallas import tpu as pltpu
from jax.sharding import PartitionSpec as P

CHUNKS = 4
STRIDE = 13
MESH = pl.DeviceIdType.MESH
VMEM_LIMIT = 56 * 1024 * 1024


def cost(flops, moved):
    return pl.CostEstimate(flops=flops, bytes_accessed=moved, transcendentals=0)


def trig(length, first, second):
    phases = (first[:, None].astype(np.int64) * second[None, :]) % length
    angles = phases.astype(np.float32) * np.float32(2.0 * math.pi / length)
    factor = np.float32(1.0 / math.sqrt(length))
    return np.cos(angles) * factor, np.sin(angles) * factor


def layout(gops, rows, width):
    per_row = width // rows
    each = -(-(per_row + 1) // (2 * gops))
    columns = []
    for g in range(gops):
        for r in range(rows):
            second = r >= rows // 2
            pair = rows - 1 - r if second else r
            for i in range(each):
                s = 2 * each * g + (each if second else 0) + i
                columns.append(per_row * pair + s if s <= per_row else -1)
    return each, np.array(columns)


def row_rows(gops, rows, width):
    each, columns = layout(gops, rows, width)
    cosine, sine = trig(width, np.maximum(columns, 0), np.arange(width))
    table = np.stack([cosine, -sine], axis=1) * (columns >= 0)[:, None, None]
    return table.reshape(2 * len(columns), width).astype(ml_dtypes.bfloat16)


def column_matrix(length, sign):
    across = np.arange(length)
    cosine, sine = trig(length, across, across)
    sine = np.float32(sign) * sine
    return np.block([[cosine, -sine], [sine, cosine]]).astype(ml_dtypes.bfloat16)


def inverse_kernel(rows_each, table_ref, b_ref, x_ref, o_ref, turned):
    turned[...] = b_ref[...].reshape(turned.shape).astype(jnp.float32)
    count = table_ref.shape[1]
    for h in range(0, rows_each, 2):
        pair = jnp.concatenate(
            [turned[pl.ds(h + d, count, stride=rows_each), :] for d in range(2)], axis=1
        ).astype(jnp.bfloat16)
        done = jnp.dot(table_ref[...], pair, preferred_element_type=jnp.float32)
        for d in range(2):
            added = x_ref[h + d].astype(jnp.float32) + done[:, 128 * d : 128 * d + 128]
            o_ref[h + d] = added.astype(jnp.bfloat16)


def inverse_rows(table, back, x):
    h, w, c = x.shape
    count = table.shape[1]
    block = 16
    return pl.pallas_call(
        functools.partial(inverse_kernel, block),
        grid=(h // block,),
        in_specs=[
            pl.BlockSpec((w, count), lambda i: (0, 0)),
            pl.BlockSpec((count, block, c), lambda i: (0, i, 0)),
            pl.BlockSpec((block, w, c), lambda i: (i, 0, 0)),
        ],
        out_specs=pl.BlockSpec((block, w, c), lambda i: (i, 0, 0)),
        out_shape=jax.ShapeDtypeStruct((h, w, c), jnp.bfloat16),
        scratch_shapes=[pltpu.VMEM((count * block, c), jnp.float32)],
        cost_estimate=cost(2 * count * w * h * c, 2 * h * c * (2 * w + count)),
        compiler_params=pltpu.CompilerParams(vmem_limit_bytes=VMEM_LIMIT),
    )(table, back, x)


def exchange_kernel(
    frames, rows, height, chunks, size, parts, fold, window,
    place_ref, anchor_ref, table_ref, x_ref, mf_ref, mi_ref, *refs,
):
    own_refs, give_refs, refs = refs[:parts], refs[parts : 2 * parts], refs[2 * parts :]
    (
        o_ref, turned, sent, slab, back, got, p_wide, n_wide, n_plain, spec, mixed,
        f_send, f_recv, a_send, a_recv, b_send, b_recv, local_sem,
    ) = refs
    devices = frames * rows
    g, r = lax.axis_index("gop"), lax.axis_index("row")
    me = g * rows + r
    second = r >= rows // 2
    short = x_ref.shape[0]
    lines = 2 * window

    def target(step):
        to = lax.rem(me + step * STRIDE, devices)
        return to, (to // rows, lax.rem(to, rows))

    barrier = pltpu.get_barrier_semaphore()

    def greet(step, carry):
        _, there = target(step)
        pl.semaphore_signal(barrier, inc=1, device_id=there, device_id_type=MESH)
        return carry

    lax.fori_loop(1, devices, greet, 0)

    def gain_copy(part):
        return pltpu.make_async_remote_copy(
            src_ref=give_refs[part], dst_ref=got.at[part],
            send_sem=f_send.at[part], recv_sem=f_recv.at[part],
            device_id=(g, rows - 1 - r), device_id_type=MESH,
        )

    def send_all(n, source, landing, send_sem, recv_sem):
        def one(step, carry):
            to, there = target(step)
            pltpu.make_async_remote_copy(
                src_ref=source.at[n, to], dst_ref=landing.at[n, me],
                send_sem=send_sem.at[n], recv_sem=recv_sem.at[n],
                device_id=there, device_id_type=MESH,
            ).start()
            return carry

        lax.fori_loop(1, devices, one, 0)

    def wait_all(n, ref, sem):
        some = ref.at[n, pl.ds(0, devices - 1)]
        pltpu.make_async_copy(some, some, sem.at[n]).wait()

    count = devices * size * 2

    def forward(n):
        for half in range(short // 16):
            def two(i, inner):
                h = half * 16 + 2 * i
                pair = jnp.concatenate([x_ref[h], x_ref[h + 1]], axis=1)
                done = jnp.dot(table_ref[n], pair, preferred_element_type=jnp.float32)
                turned[pl.ds(2 * i, count, stride=16), :] = done[:, :128]
                turned[pl.ds(2 * i + 1, count, stride=16), :] = done[:, 128:]
                return inner

            lax.fori_loop(0, 8, two, 0, unroll=True)
            sent[n, :, :, pl.ds(half * 16, 16), :] = (
                turned[...].astype(jnp.bfloat16).reshape(devices, 2 * size, 16, 128)
            )

    def send_forward(n):
        send_all(n, sent, slab, a_send, a_recv)
        slab[n, me] = sent[n, me]

    def later(n, carry):
        forward(n)
        send_forward(n)
        return carry

    forward(0)
    pl.semaphore_wait(barrier, devices - 1)
    for part in range(parts):
        gain_copy(part).start()
        if part == 0:
            send_forward(0)
        lax.fori_loop(max(1, part * fold), (part + 1) * fold, later, 0)

    def load_gains(part):
        gain_copy(part).wait()
        block = 512

        def widen(i, carry):
            at = pl.ds(pl.multiple_of(i * block, block), block)
            own = own_refs[part][at, :].astype(jnp.float32)
            other = got[part, at, :].astype(jnp.float32)
            p_wide[at, :] = jnp.where(second, other, own)
            n_plain[at, :] = jnp.where(second, own, other)
            return carry

        lax.fori_loop(0, 3 * height * lines // block, widen, 0)

        def mirror(k, carry):
            there = lax.rem(height - k, height)
            for j in range(3):
                to = pl.ds(pl.multiple_of((j * height + k) * lines, lines), lines)
                at = pl.ds(pl.multiple_of((j * height + there) * lines, lines), lines)
                n_wide[to, :] = n_plain[at, :]
            return carry

        lax.fori_loop(0, height, mirror, 0)

    def middle(n, carry):
        for part in range(parts):
            @pl.when(n == part * fold)
            def _():
                load_gains(part)

        wait_all(n, slab, a_recv)

        def one_slot(i, inner):
            slot = n * size + i
            for f in range(0, frames, 2):
                sides = [
                    jnp.concatenate(
                        [slab[n, (f + d) * rows + k, 2 * i + q] for q in range(2) for k in range(rows)],
                        axis=0,
                    )
                    for d in range(2)
                ]
                done = jnp.dot(
                    mf_ref[...], jnp.concatenate(sides, axis=1), preferred_element_type=jnp.float32
                ).astype(jnp.bfloat16)
                spec[f] = done[:, :128]
                spec[f + 1] = done[:, 128:]

            place_p, place_n = place_ref[0, slot], place_ref[1, slot]
            weight_p = place_ref[2, slot].astype(jnp.float32)
            weight_n = place_ref[3, slot].astype(jnp.float32)
            chunk = 32

            def mix(step, deep):
                k = pl.multiple_of(step * chunk, chunk)
                gains = []
                for j in range(3):
                    pieces = []
                    for p in range(2):
                        start = (j * height + k) * lines + p * window
                        right = p_wide[pl.ds(start + place_p, chunk, stride=lines), :]
                        left = n_wide[pl.ds(start + place_n, chunk, stride=lines), :]
                        left = left * weight_n
                        pieces.append(right * weight_p + (left if p == 0 else -left))
                    gains.append(pieces)
                for f in range(frames):
                    real, imag = None, None
                    for j in range(3):
                        source = f if j == 0 else anchor_ref[f, j - 1]
                        s_real = spec[source, pl.ds(k, chunk), :].astype(jnp.float32)
                        s_imag = spec[source, pl.ds(height + k, chunk), :].astype(jnp.float32)
                        g_real, g_imag = gains[j]
                        new_real = g_real * s_real - g_imag * s_imag
                        new_imag = g_real * s_imag + g_imag * s_real
                        real = new_real if real is None else real + new_real
                        imag = new_imag if imag is None else imag + new_imag
                    lanes = pl.ds(f * 128, 128)
                    mixed[pl.ds(k, chunk), lanes] = real.astype(jnp.bfloat16)
                    mixed[pl.ds(height + k, chunk), lanes] = imag.astype(jnp.bfloat16)
                return deep

            lax.fori_loop(0, height // chunk, mix, 0)

            for f in range(0, frames, 2):
                done = jnp.dot(
                    mi_ref[...], mixed[:, 128 * f : 128 * f + 256],
                    preferred_element_type=jnp.float32,
                ).astype(jnp.bfloat16)
                for d in range(2):
                    for q in range(2):
                        for k in range(rows):
                            at = q * height + k * short
                            back[n, (f + d) * rows + k, 2 * i + q] = done[
                                at : at + short, 128 * d : 128 * d + 128
                            ]
            return inner

        lax.fori_loop(0, size, one_slot, 0)
        send_all(n, back, o_ref, b_send, b_recv)
        pltpu.make_async_copy(back.at[n, me], o_ref.at[n, me], local_sem.at[n]).start()
        return carry

    lax.fori_loop(0, chunks, middle, 0)

    def finish(n, carry):
        wait_all(n, sent, a_send)
        wait_all(n, back, b_send)
        wait_all(n, o_ref, b_recv)
        pltpu.make_async_copy(back.at[n, me], o_ref.at[n, me], local_sem.at[n]).wait()
        return carry

    lax.fori_loop(0, chunks, finish, 0)


def exchange(frames, rows, height, size, fold, window, place, anchors, table, x, own, give, mf, mi):
    chunks, count, w = table.shape
    h, _, c = x.shape
    devices = frames * rows
    parts = len(own)
    shape = (chunks, devices, 2 * size, h, c)
    smem = pl.BlockSpec(memory_space=pltpu.SMEM)
    vmem = pl.BlockSpec(memory_space=pltpu.VMEM)
    hbm = pl.BlockSpec(memory_space=pl.ANY)
    wide = pltpu.VMEM(own[0].shape, jnp.float32)
    dma = pltpu.SemaphoreType.DMA
    return pl.pallas_call(
        functools.partial(exchange_kernel, frames, rows, height, chunks, size, parts, fold, window),
        in_specs=[smem, smem, vmem, vmem, vmem, vmem, *[vmem] * parts, *[hbm] * parts],
        out_specs=hbm,
        out_shape=jax.ShapeDtypeStruct(shape, jnp.bfloat16),
        scratch_shapes=[
            pltpu.VMEM((count * 16, c), jnp.float32),
            *[pltpu.VMEM(shape, jnp.bfloat16)] * 3,
            pltpu.VMEM((parts, *own[0].shape), jnp.bfloat16),
            wide, wide, wide,
            pltpu.VMEM((frames, 2 * height, c), jnp.bfloat16),
            pltpu.VMEM((2 * height, frames * c), jnp.bfloat16),
            dma((parts,)), dma((parts,)),
            *[dma((chunks,))] * 5,
        ],
        cost_estimate=cost(8 * height * x.size, 4 * x.size + 4 * parts * own[0].size),
        compiler_params=pltpu.CompilerParams(
            vmem_limit_bytes=VMEM_LIMIT, collective_id=0, has_side_effects=True
        ),
    )(place, anchors, table, x, mf, mi, *own, *give)


def on_device(gops, rows, features, filters, anchors):
    h, w, c = features.shape[1:]
    height = filters.shape[1]
    per_row = filters.shape[3]
    devices = gops * rows
    table = row_rows(gops, rows, w)
    each, _ = layout(gops, rows, w)
    g, r = lax.axis_index("gop"), lax.axis_index("row")
    second = r >= rows // 2
    window = 4
    parts = max(1, each // window)
    part_size = each // parts
    chunks = math.gcd(CHUNKS, each)
    size = each // chunks
    limit = per_row - window
    cut = lambda start: lax.dynamic_slice_in_dim(filters, start, window, 3).reshape(-1, c)
    tables = table.reshape(devices, chunks, 2 * size, w).swapaxes(0, 1).reshape(chunks, -1, w)

    def starts(s, clip):
        return clip(s, 0, limit), clip(per_row - s - part_size + 1, 0, limit)

    places = np.zeros((devices, 4, each), np.int32)
    for at in range(devices):
        first = 2 * each * (at // rows) + (each if at % rows >= rows // 2 else 0)
        for i in range(each):
            s = first + i
            plus, minus = starts(first + i // part_size * part_size, np.clip)
            inside = np.clip([s - plus, per_row - s - minus], 0, window - 1)
            places[at, :, i] = [*inside, s < per_row, 1 <= s <= per_row]
    place = lax.dynamic_index_in_dim(jnp.asarray(places), g * rows + r, 0, keepdims=False)
    first_slot = 2 * each * g + jnp.where(second, each, 0)
    first_theirs = 2 * each * g + jnp.where(second, 0, each)
    give, own = [], []
    for n in range(parts):
        plus, minus = starts(first_theirs + n * part_size, jnp.clip)
        give.append(cut(jnp.where(second, minus, plus)))
        plus, minus = starts(first_slot + n * part_size, jnp.clip)
        own.append(cut(jnp.where(second, minus, plus)))
    back = exchange(
        gops, rows, height, size, part_size // size, window, place, anchors,
        jnp.asarray(tables), features[0], own, give,
        jnp.asarray(column_matrix(height, -1.0)), jnp.asarray(column_matrix(height, 1.0)),
    )
    table_back = jnp.asarray(np.ascontiguousarray(tables.reshape(-1, w).T))
    return inverse_rows(table_back, back.reshape(-1, h, c), features[0])[None]


def solution(mesh):
    in_specs = (P("gop", "row", None, None), P(None, None, None, "row", None), P())
    out_specs = P("gop", "row", None, None)
    return jax.shard_map(
        functools.partial(on_device, mesh.shape["gop"], mesh.shape["row"]),
        mesh=mesh, in_specs=in_specs, out_specs=out_specs, check_vma=False,
    )
```

```python
import functools
import math

import jax
import jax.numpy as jnp
import ml_dtypes
import numpy as np
from jax import lax
from jax.experimental import pallas as pl
from jax.experimental.pallas import tpu as pltpu
from jax.sharding import PartitionSpec as P

CHUNKS = 8
STRIDE = 13
MESH = pl.DeviceIdType.MESH
VMEM_LIMIT = 56 * 1024 * 1024


def cost(flops, moved):
    return pl.CostEstimate(flops=flops, bytes_accessed=moved, transcendentals=0)


def trig(length, first, second):
    phases = (first[:, None].astype(np.int64) * second[None, :]) % length
    angles = phases.astype(np.float32) * np.float32(2.0 * math.pi / length)
    factor = np.float32(1.0 / math.sqrt(length))
    return np.cos(angles) * factor, np.sin(angles) * factor


def layout(gops, rows, width):
    per_row = width // rows
    each = -(-(per_row + 1) // (2 * gops))
    columns = []
    for g in range(gops):
        for r in range(rows):
            second = r >= rows // 2
            pair = rows - 1 - r if second else r
            for i in range(each):
                s = 2 * each * g + (each if second else 0) + i
                columns.append(per_row * pair + s if s <= per_row else -1)
    return each, np.array(columns)


def row_rows(gops, rows, width):
    each, columns = layout(gops, rows, width)
    cosine, sine = trig(width, np.maximum(columns, 0), np.arange(width))
    table = np.stack([cosine, -sine], axis=1) * (columns >= 0)[:, None, None]
    return table.reshape(2 * len(columns), width).astype(ml_dtypes.bfloat16)


def column_matrix(length, sign):
    across = np.arange(length)
    cosine, sine = trig(length, across, across)
    sine = np.float32(sign) * sine
    return np.block([[cosine, -sine], [sine, cosine]]).astype(ml_dtypes.bfloat16)


def inverse_kernel(rows_each, table_ref, b_ref, x_ref, o_ref, turned):
    turned[...] = b_ref[...].reshape(turned.shape).astype(jnp.float32)
    count = table_ref.shape[1]
    for h in range(0, rows_each, 2):
        pair = jnp.concatenate(
            [turned[pl.ds(h + d, count, stride=rows_each), :] for d in range(2)], axis=1
        ).astype(jnp.bfloat16)
        done = jnp.dot(table_ref[...], pair, preferred_element_type=jnp.float32)
        for d in range(2):
            added = x_ref[h + d].astype(jnp.float32) + done[:, 128 * d : 128 * d + 128]
            o_ref[h + d] = added.astype(jnp.bfloat16)


def inverse_rows(table, back, x):
    h, w, c = x.shape
    count = table.shape[1]
    block = 16
    return pl.pallas_call(
        functools.partial(inverse_kernel, block),
        grid=(h // block,),
        in_specs=[
            pl.BlockSpec((w, count), lambda i: (0, 0)),
            pl.BlockSpec((count, block, c), lambda i: (0, i, 0)),
            pl.BlockSpec((block, w, c), lambda i: (i, 0, 0)),
        ],
        out_specs=pl.BlockSpec((block, w, c), lambda i: (i, 0, 0)),
        out_shape=jax.ShapeDtypeStruct((h, w, c), jnp.bfloat16),
        scratch_shapes=[pltpu.VMEM((count * block, c), jnp.float32)],
        cost_estimate=cost(2 * count * w * h * c, 2 * h * c * (2 * w + count)),
        compiler_params=pltpu.CompilerParams(vmem_limit_bytes=VMEM_LIMIT),
    )(table, back, x)


def exchange_kernel(
    frames, rows, height, chunks, size, parts, fold, window,
    place_ref, anchor_ref, table_ref, x_ref, mf_ref, mi_ref, *refs,
):
    own_refs, give_refs, refs = refs[:parts], refs[parts : 2 * parts], refs[2 * parts :]
    (
        o_ref, turned, sent, slab, back, got, p_wide, n_wide, n_plain, spec, mixed,
        f_send, f_recv, a_send, a_recv, b_send, b_recv, local_sem,
    ) = refs
    devices = frames * rows
    g, r = lax.axis_index("gop"), lax.axis_index("row")
    me = g * rows + r
    second = r >= rows // 2
    short = x_ref.shape[0]
    lines = 2 * window

    def target(step):
        to = lax.rem(me + step * STRIDE, devices)
        return to, (to // rows, lax.rem(to, rows))

    barrier = pltpu.get_barrier_semaphore()

    def greet(step, carry):
        _, there = target(step)
        pl.semaphore_signal(barrier, inc=1, device_id=there, device_id_type=MESH)
        return carry

    lax.fori_loop(1, devices, greet, 0)

    def gain_copy(part):
        return pltpu.make_async_remote_copy(
            src_ref=give_refs[part], dst_ref=got.at[part],
            send_sem=f_send.at[part], recv_sem=f_recv.at[part],
            device_id=(g, rows - 1 - r), device_id_type=MESH,
        )

    def send_all(n, source, landing, send_sem, recv_sem):
        def one(step, carry):
            to, there = target(step)
            pltpu.make_async_remote_copy(
                src_ref=source.at[n, to], dst_ref=landing.at[n, me],
                send_sem=send_sem.at[n], recv_sem=recv_sem.at[n],
                device_id=there, device_id_type=MESH,
            ).start()
            return carry

        lax.fori_loop(1, devices, one, 0)

    def wait_all(n, ref, sem):
        some = ref.at[n, pl.ds(0, devices - 1)]
        pltpu.make_async_copy(some, some, sem.at[n]).wait()

    count = devices * size * 2

    def forward(n):
        for half in range(short // 16):
            def two(i, inner):
                h = half * 16 + 2 * i
                pair = jnp.concatenate([x_ref[h], x_ref[h + 1]], axis=1)
                done = jnp.dot(table_ref[n], pair, preferred_element_type=jnp.float32)
                turned[pl.ds(2 * i, count, stride=16), :] = done[:, :128]
                turned[pl.ds(2 * i + 1, count, stride=16), :] = done[:, 128:]
                return inner

            lax.fori_loop(0, 8, two, 0, unroll=True)
            sent[n, :, :, pl.ds(half * 16, 16), :] = (
                turned[...].astype(jnp.bfloat16).reshape(devices, 2 * size, 16, 128)
            )

    def send_forward(n):
        send_all(n, sent, slab, a_send, a_recv)
        slab[n, me] = sent[n, me]

    def later(n, carry):
        forward(n)
        send_forward(n)
        return carry

    forward(0)
    pl.semaphore_wait(barrier, devices - 1)
    for part in range(parts):
        gain_copy(part).start()
        if part == 0:
            send_forward(0)
        lax.fori_loop(max(1, part * fold), (part + 1) * fold, later, 0)

    def load_gains(part):
        gain_copy(part).wait()
        block = 512

        def widen(i, carry):
            at = pl.ds(pl.multiple_of(i * block, block), block)
            own = own_refs[part][at, :].astype(jnp.float32)
            other = got[part, at, :].astype(jnp.float32)
            p_wide[at, :] = jnp.where(second, other, own)
            n_plain[at, :] = jnp.where(second, own, other)
            return carry

        lax.fori_loop(0, 3 * height * lines // block, widen, 0)

        def mirror(k, carry):
            there = lax.rem(height - k, height)
            for j in range(3):
                to = pl.ds(pl.multiple_of((j * height + k) * lines, lines), lines)
                at = pl.ds(pl.multiple_of((j * height + there) * lines, lines), lines)
                n_wide[to, :] = n_plain[at, :]
            return carry

        lax.fori_loop(0, height, mirror, 0)

    def middle(n, carry):
        for part in range(parts):
            @pl.when(n == part * fold)
            def _():
                load_gains(part)

        wait_all(n, slab, a_recv)

        def one_slot(i, inner):
            slot = n * size + i
            for f in range(0, frames, 2):
                sides = [
                    jnp.concatenate(
                        [slab[n, (f + d) * rows + k, 2 * i + q] for q in range(2) for k in range(rows)],
                        axis=0,
                    )
                    for d in range(2)
                ]
                done = jnp.dot(
                    mf_ref[...], jnp.concatenate(sides, axis=1), preferred_element_type=jnp.float32
                ).astype(jnp.bfloat16)
                spec[f] = done[:, :128]
                spec[f + 1] = done[:, 128:]

            place_p, place_n = place_ref[0, slot], place_ref[1, slot]
            weight_p = place_ref[2, slot].astype(jnp.float32)
            weight_n = place_ref[3, slot].astype(jnp.float32)
            chunk = 32

            def mix(step, deep):
                k = pl.multiple_of(step * chunk, chunk)
                gains = []
                for j in range(3):
                    pieces = []
                    for p in range(2):
                        start = (j * height + k) * lines + p
                        right = p_wide[pl.ds(start + 2 * place_p, chunk, stride=lines), :]
                        left = n_wide[pl.ds(start + 2 * place_n, chunk, stride=lines), :]
                        left = left * weight_n
                        pieces.append(right * weight_p + (left if p == 0 else -left))
                    gains.append(pieces)
                for f in range(frames):
                    real, imag = None, None
                    for j in range(3):
                        source = f if j == 0 else anchor_ref[f, j - 1]
                        s_real = spec[source, pl.ds(k, chunk), :].astype(jnp.float32)
                        s_imag = spec[source, pl.ds(height + k, chunk), :].astype(jnp.float32)
                        g_real, g_imag = gains[j]
                        new_real = g_real * s_real - g_imag * s_imag
                        new_imag = g_real * s_imag + g_imag * s_real
                        real = new_real if real is None else real + new_real
                        imag = new_imag if imag is None else imag + new_imag
                    lanes = pl.ds(f * 128, 128)
                    mixed[pl.ds(k, chunk), lanes] = real.astype(jnp.bfloat16)
                    mixed[pl.ds(height + k, chunk), lanes] = imag.astype(jnp.bfloat16)
                return deep

            lax.fori_loop(0, height // chunk, mix, 0)

            for f in range(0, frames, 2):
                done = jnp.dot(
                    mi_ref[...], mixed[:, 128 * f : 128 * f + 256],
                    preferred_element_type=jnp.float32,
                ).astype(jnp.bfloat16)
                for d in range(2):
                    for q in range(2):
                        for k in range(rows):
                            at = q * height + k * short
                            back[n, (f + d) * rows + k, 2 * i + q] = done[
                                at : at + short, 128 * d : 128 * d + 128
                            ]
            return inner

        lax.fori_loop(0, size, one_slot, 0)
        send_all(n, back, o_ref, b_send, b_recv)
        pltpu.make_async_copy(back.at[n, me], o_ref.at[n, me], local_sem.at[n]).start()
        return carry

    lax.fori_loop(0, chunks, middle, 0)

    def finish(n, carry):
        wait_all(n, sent, a_send)
        wait_all(n, back, b_send)
        wait_all(n, o_ref, b_recv)
        pltpu.make_async_copy(back.at[n, me], o_ref.at[n, me], local_sem.at[n]).wait()
        return carry

    lax.fori_loop(0, chunks, finish, 0)


def exchange(frames, rows, height, size, fold, window, place, anchors, table, x, own, give, mf, mi):
    chunks, count, w = table.shape
    h, _, c = x.shape
    devices = frames * rows
    parts = len(own)
    shape = (chunks, devices, 2 * size, h, c)
    smem = pl.BlockSpec(memory_space=pltpu.SMEM)
    vmem = pl.BlockSpec(memory_space=pltpu.VMEM)
    hbm = pl.BlockSpec(memory_space=pl.ANY)
    wide = pltpu.VMEM(own[0].shape, jnp.float32)
    dma = pltpu.SemaphoreType.DMA
    return pl.pallas_call(
        functools.partial(exchange_kernel, frames, rows, height, chunks, size, parts, fold, window),
        in_specs=[smem, smem, vmem, vmem, vmem, vmem, *[vmem] * parts, *[hbm] * parts],
        out_specs=hbm,
        out_shape=jax.ShapeDtypeStruct(shape, jnp.bfloat16),
        scratch_shapes=[
            pltpu.VMEM((count * 16, c), jnp.float32),
            *[pltpu.VMEM(shape, jnp.bfloat16)] * 3,
            pltpu.VMEM((parts, *own[0].shape), jnp.bfloat16),
            wide, wide, wide,
            pltpu.VMEM((frames, 2 * height, c), jnp.bfloat16),
            pltpu.VMEM((2 * height, frames * c), jnp.bfloat16),
            dma((parts,)), dma((parts,)),
            *[dma((chunks,))] * 5,
        ],
        cost_estimate=cost(8 * height * x.size, 4 * x.size + 4 * parts * own[0].size),
        compiler_params=pltpu.CompilerParams(
            vmem_limit_bytes=VMEM_LIMIT, collective_id=0, has_side_effects=True
        ),
    )(place, anchors, table, x, mf, mi, *own, *give)


def on_device(gops, rows, features, filters, anchors):
    h, w, c = features.shape[1:]
    height = filters.shape[1]
    per_row = filters.shape[3]
    devices = gops * rows
    table = row_rows(gops, rows, w)
    each, _ = layout(gops, rows, w)
    g, r = lax.axis_index("gop"), lax.axis_index("row")
    second = r >= rows // 2
    window = 4
    parts = max(1, each // window)
    part_size = each // parts
    chunks = math.gcd(CHUNKS, each)
    size = each // chunks
    limit = per_row - window
    cut = lambda start: (
        lax.dynamic_slice_in_dim(filters, start, window, 3).swapaxes(2, 3).reshape(-1, c)
    )
    tables = table.reshape(devices, chunks, 2 * size, w).swapaxes(0, 1).reshape(chunks, -1, w)

    def starts(s, clip):
        return clip(s, 0, limit), clip(per_row - s - part_size + 1, 0, limit)

    places = np.zeros((devices, 4, each), np.int32)
    for at in range(devices):
        first = 2 * each * (at // rows) + (each if at % rows >= rows // 2 else 0)
        for i in range(each):
            s = first + i
            plus, minus = starts(first + i // part_size * part_size, np.clip)
            inside = np.clip([s - plus, per_row - s - minus], 0, window - 1)
            places[at, :, i] = [*inside, s < per_row, 1 <= s <= per_row]
    place = lax.dynamic_index_in_dim(jnp.asarray(places), g * rows + r, 0, keepdims=False)
    first_slot = 2 * each * g + jnp.where(second, each, 0)
    first_theirs = 2 * each * g + jnp.where(second, 0, each)
    give, own = [], []
    for n in range(parts):
        plus, minus = starts(first_theirs + n * part_size, jnp.clip)
        give.append(cut(jnp.where(second, minus, plus)))
        plus, minus = starts(first_slot + n * part_size, jnp.clip)
        own.append(cut(jnp.where(second, minus, plus)))
    back = exchange(
        gops, rows, height, size, part_size // size, window, place, anchors,
        jnp.asarray(tables), features[0], own, give,
        jnp.asarray(column_matrix(height, -1.0)), jnp.asarray(column_matrix(height, 1.0)),
    )
    table_back = jnp.asarray(np.ascontiguousarray(tables.reshape(-1, w).T))
    return inverse_rows(table_back, back.reshape(-1, h, c), features[0])[None]


def solution(mesh):
    in_specs = (P("gop", "row", None, None), P(None, None, None, "row", None), P())
    out_specs = P("gop", "row", None, None)
    return jax.shard_map(
        functools.partial(on_device, mesh.shape["gop"], mesh.shape["row"]),
        mesh=mesh, in_specs=in_specs, out_specs=out_specs, check_vma=False,
    )
```
